256 devices in a mesh: dp: 16 (over x, y), ctx: 16 (over z, core).
Axes of the slice: x: 4, y: 4, z: 8, core: 2. Of those that a mesh axis runs over, the one named last changes fastest.
Arguments:
- queries: bfloat16 [524288, 1024], P(('dp', 'ctx')), parts along dimension 0, as said below
- keys: bfloat16 [524288, 128], P(('dp', 'ctx')), parts along dimension 0, as said below
- values: bfloat16 [524288, 128], P(('dp', 'ctx')), parts along dimension 0, may hold values from -6 to 6
- doc_lengths: int32 [1024], P('dp'), parts along dimension 0, may hold values from 1 to 1024, 32768 in all
- tile_owner: int32 [4096], P('dp'), parts along dimension 0, may hold values from 0 to 255, as said below
Outputs:
- attended: bfloat16 [524288, 1024], P(('dp', 'ctx')), parts along dimension 0
The draws below stay inside these ranges and needn't reach their ends.
There are 16 independent parts, one for each index of `dp`. The reference program is written for one: setup_inputs(seed, part) draws one part's arguments, and reference() takes and returns one part's arrays. A program takes and returns all parts, laid end to end along the dimension named above; each array names one. Nothing has to cross between parts.
Inputs may be any that keep to these rules, and one draw needn't show every extreme that they name: `queries`: entries lie within -8 to 8. `keys`: entries lie within -8 to 8. `doc_lengths`: they sum to 32768; the largest is exactly 1024. `tile_owner`: A permutation of the 256 tiles. For owner o, source s and 0 <= j < 1, position o * 16 + s + j holds a tile of the rows that device s holds in the even layout, that is a tile from s * 16 to s * 16 + 15.
All inputs are finite; a program needn't handle non-finite values.
Results may differ from the reference program's by a relative error of at most 0.0037.
Values may be sent and summed in bfloat16 or wider, within the bound.
A program may use at most 128 MiB of HBM per device.

```python
import math
import jax
import jax.numpy as jnp
import numpy as np
from jax import lax

DH = 128
HEADS = 8
TILE = 128
DOC_MOST = 1024
SEQ = 32768
TILES = 256
NDOCS = 64
N_CTX = 16


def draw_queries(key, part):
    key = jax.random.fold_in(key, 1)
    field = jax.random.truncated_normal(key, -8.0, 8.0, (SEQ, HEADS * DH), jnp.float32)
    return field.astype(jnp.bfloat16)


def draw_keys(key, part):
    key = jax.random.fold_in(key, 2)
    field = jax.random.truncated_normal(key, -8.0, 8.0, (SEQ, DH), jnp.float32)
    return field.astype(jnp.bfloat16)


def draw_tile_owner(key, part):
    key = jax.random.fold_in(key, 3)
    count = N_CTX
    per_dev = TILES // count
    per_peer = per_dev // count
    sources = jax.random.split(key, count)
    orders = jax.vmap(lambda single: jax.random.permutation(single, per_dev))(sources)
    orders = orders.reshape(count, count, per_peer)
    offsets = (jnp.arange(count, dtype=jnp.int32) * per_dev)[:, None, None]
    placed = (orders.astype(jnp.int32) + offsets).transpose(1, 0, 2)
    return placed.reshape(TILES).astype(jnp.int32)


def levels(stream_key, shape, cuts, smallest, top_value):
    gain, own = 1.0, jax.random.fold_in(stream_key, 6)
    for axis_at, shards_of in cuts:
        draws = jnp.exp(jax.random.uniform(jax.random.fold_in(own, axis_at), (shards_of,), jnp.float32, smallest / len(cuts), top_value / len(cuts)))
        gain = gain * jnp.repeat(draws, shape[axis_at] // shards_of).reshape([-1 if axis == axis_at else 1 for axis in range(len(shape))])
    return gain


def split_up(count, total, most, slope):
    weights = [(1 << 20) // math.isqrt(grade ** slope) + 1 for grade in range(2, count + 1)]
    spare, given = total - most - (count - 1), [1] * (count - 1)
    while spare > 0:
        movable = [i for i in range(count - 1) if given[i] < most]
        pool, remaining = sum([weights[i] for i in movable]), spare
        for i in movable:
            more = min(most - given[i], max(1, remaining * weights[i] // pool), spare)
            given[i] = given[i] + more
            spare = spare - more
    return np.array([most] + given)


def ragged(own_key, number_of, total, limit, slope):
    if number_of == 2:
        one = jax.random.randint(own_key, (), max(1, total - limit), min(limit, total - 1) + 1)
        return jnp.stack([one, total - one])
    sizes = jnp.asarray(split_up(number_of, total, limit, slope), jnp.int32)
    couples = (number_of - 1) // 2
    donor, sink = sizes[1:1 + 2 * couples:2], sizes[2:2 + 2 * couples:2]
    slack = jnp.minimum(donor - 1, limit - sink)
    moved = jax.random.randint(jax.random.fold_in(own_key, 1), (couples,), 0, 1 << 20) % (slack + 1)
    sizes = sizes.at[1:1 + 2 * couples:2].set(donor - moved).at[2:2 + 2 * couples:2].set(sink + moved)
    return sizes[jax.random.permutation(jax.random.fold_in(own_key, 2), number_of)]


def normal_values(key, extent, deviation, most, shards=(), held_as=jnp.bfloat16):
    values = deviation * jax.random.normal(key, extent, jnp.float32)
    if shards:
        values = values * levels(key, extent, shards, -0.22, 0.18)
    return jnp.clip(values, -most, most).astype(held_as)


def setup_inputs(seed: int = 0, part: int = 0) -> dict:
    streams_of = jax.random.split(jax.random.key(seed), 6)
    part_splits = jax.random.split(jax.random.fold_in(streams_of[5], part), 6)
    queries = draw_queries(jax.random.fold_in(jax.random.fold_in(streams_of[5], part), 71), part)
    keys = draw_keys(jax.random.fold_in(jax.random.fold_in(streams_of[5], part), 71), part)
    values = normal_values(part_splits[2], (SEQ, DH), 1.0, 6.0, ((0, 16),))
    doc_lengths = ragged(part_splits[3], NDOCS, SEQ, DOC_MOST, 2).astype(jnp.int32)
    tile_owner = draw_tile_owner(jax.random.fold_in(jax.random.fold_in(streams_of[5], part), 71), part)
    return {"queries": queries, "keys": keys, "values": values, "doc_lengths": doc_lengths, "tile_owner": tile_owner}


def doc_index(positions, ends):
    return jnp.sum((ends[None, :] <= positions[:, None]).astype(jnp.int32), axis=1)


def attend_tile(q_tile, key_win, val_win, start, ends):
    tile_rows = q_tile.shape[0]
    span = key_win.shape[0]
    head_dim = key_win.shape[1]
    heads = q_tile.shape[1] // head_dim
    row_pos = start + jnp.arange(tile_rows, dtype=jnp.int32)
    key_pos = start - DOC_MOST + jnp.arange(span, dtype=jnp.int32)
    allowed = (key_pos[None, :] >= 0) & (key_pos[None, :] <= row_pos[:, None])
    allowed = allowed & (doc_index(key_pos, ends)[None, :] == doc_index(row_pos, ends)[:, None])
    flat_q = q_tile.reshape(tile_rows * heads, head_dim)
    scores = jnp.dot(flat_q, key_win.T, preferred_element_type=jnp.float32) * (head_dim ** -0.5)
    scores = scores.reshape(tile_rows, heads, span)
    scores = jnp.where(allowed[:, None, :], scores, -jnp.inf)
    peak = jnp.max(scores, axis=-1, keepdims=True)
    weights = jnp.exp(scores - peak)
    total = jnp.sum(weights, axis=-1, keepdims=True)
    probs = weights.astype(jnp.bfloat16).reshape(tile_rows * heads, span)
    mixed = jnp.dot(probs, val_win, preferred_element_type=jnp.float32).reshape(tile_rows, heads, head_dim)
    return (mixed / total).astype(jnp.bfloat16).reshape(tile_rows, heads * head_dim)


def reference(queries, keys, values, doc_lengths, tile_owner):
    ends = jnp.cumsum(doc_lengths).astype(jnp.int32)
    blank = jnp.zeros((DOC_MOST, DH), keys.dtype)
    key_buf = jnp.concatenate([blank, keys], axis=0)
    val_buf = jnp.concatenate([blank, values], axis=0)
    q_tiles = queries.reshape(TILES, TILE, HEADS * DH)

    def one_tile(position):
        source = tile_owner[position].astype(jnp.int32)
        start = (source * TILE).astype(jnp.int32)
        q_tile = lax.dynamic_index_in_dim(q_tiles, source, 0, keepdims=False)
        key_win = lax.dynamic_slice_in_dim(key_buf, start, DOC_MOST + TILE, 0)
        val_win = lax.dynamic_slice_in_dim(val_buf, start, DOC_MOST + TILE, 0)
        return attend_tile(q_tile, key_win, val_win, start, ends)

    result = lax.map(one_tile, jnp.arange(TILES, dtype=jnp.int32))
    return result.reshape(SEQ, HEADS * DH)
```

```python
import functools

import jax
import jax.numpy as jnp
from jax import lax
from jax.experimental import pallas as pl
from jax.experimental.pallas import tpu as pltpu
from jax.sharding import PartitionSpec as P

TILE = 128
DOC_MOST = 1024
DH = 128
MESH = pl.DeviceIdType.MESH
LOG2E = 1.4426950408889634
MASKED = -1e30


def kernel(
    n, tiles, heads, pair, q_hbm, k_hbm, v_hbm, len_ref, owner_ref, out_hbm,
    q_all, k_ext, v_ext, stage, bias, local_sem, halo_send, halo_recv, send_sem, recv_sem,
):
    dp = lax.axis_index("dp")
    me = lax.axis_index("ctx")
    tokens = tiles * TILE
    window = DOC_MOST + TILE
    reach = DOC_MOST // TILE

    loads = [
        pltpu.make_async_copy(q_hbm, q_all, local_sem.at[0]),
        pltpu.make_async_copy(k_hbm, k_ext.at[pl.ds(reach, tiles)], local_sem.at[1]),
        pltpu.make_async_copy(v_hbm, v_ext.at[pl.ds(reach, tiles)], local_sem.at[2]),
    ]
    for load in loads:
        load.start()

    barrier = pltpu.get_barrier_semaphore()
    for step in range(1, n):
        pl.semaphore_signal(
            barrier, inc=1, device_id=(dp, lax.rem(me + step, n)), device_id_type=MESH
        )
    pl.semaphore_wait(barrier, n - 1)

    following = (dp, lax.rem(me + 1, n))
    halos = [
        pltpu.make_async_remote_copy(
            src_ref=src.at[pl.ds(tiles - reach, reach)],
            dst_ref=dst.at[pl.ds(0, reach)],
            send_sem=halo_send.at[at],
            recv_sem=halo_recv.at[at],
            device_id=following,
            device_id_type=MESH,
        )
        for at, (src, dst) in enumerate(((k_hbm, k_ext), (v_hbm, v_ext)))
    ]
    for halo in halos:
        halo.start()

    lane = lax.broadcasted_iota(jnp.int32, (8, 128), 1)

    run, ends = jnp.int32(0), jnp.full((8, 128), 1 << 24, jnp.int32)
    for doc in range(len_ref.shape[0]):
        run = run + len_ref[doc]
        ends = jnp.where(lane == doc, run, ends)
    ends = ends.astype(jnp.float32)[0:1, :]

    for load in loads:
        load.wait()
    for halo in halos:
        halo.wait()

    row_in = lax.broadcasted_iota(jnp.int32, (TILE, 128), 0)
    key_at = lax.broadcasted_iota(jnp.int32, (TILE, window), 1) - DOC_MOST
    row_at = lax.broadcasted_iota(jnp.int32, (TILE, window), 0)

    def target(step):
        j = step // 2
        dz = (4 - (j + 1) // 2) * (1 - 2 * ((j + 1) % 2))
        return ((me // 2 + dz + n // 2) % (n // 2)) * 2 + (me % 2 + 1 + step % 2) % 2

    def remote(step):
        return pltpu.make_async_remote_copy(
            src_ref=stage.at[step],
            dst_ref=out_hbm.at[pl.ds(me * TILE, TILE)],
            send_sem=send_sem.at[step],
            recv_sem=recv_sem.at[step],
            device_id=(dp, target(step)),
            device_id_type=MESH,
        )

    own = pltpu.make_async_copy(
        stage.at[n - 1], out_hbm.at[pl.ds(me * TILE, TILE)], local_sem.at[3]
    )

    def one_tile(step, carry):
        tile = lax.rem(owner_ref[target(step) * n + me], tiles)
        base = (me * tokens + tile * TILE).astype(jnp.float32)
        begin = jnp.max(
            jnp.where(ends <= row_in.astype(jnp.float32) + base, ends, 0.0),
            axis=1, keepdims=True,
        )
        seen = (key_at <= row_at) & (key_at.astype(jnp.float32) + base >= begin)
        bias[...] = jnp.where(seen, 0.0, MASKED)

        for group in range(heads // pair):
            at = [(group * pair + h) * DH for h in range(pair)]
            q = jnp.concatenate([q_all[tile, :, pl.ds(a, DH)] for a in at], axis=0)
            k = jnp.concatenate([k_ext[tile + b] for b in range(reach + 1)], axis=0)
            v = jnp.concatenate([v_ext[tile + b] for b in range(reach + 1)], axis=0)
            scores = lax.dot_general(
                q, k, (((1,), (1,)), ((), ())), preferred_element_type=jnp.float32
            )
            scores = scores * (LOG2E * DH ** -0.5) + jnp.concatenate([bias[...]] * pair, axis=0)
            peak = jnp.max(scores, axis=1, keepdims=True)
            weights = jnp.exp2(scores - peak)
            total = jnp.sum(weights, axis=1, keepdims=True)
            mixed = jnp.dot(weights.astype(jnp.bfloat16), v, preferred_element_type=jnp.float32)
            mixed = (mixed / total).astype(jnp.bfloat16)
            for h, a in enumerate(at):
                stage[step, :, pl.ds(a, DH)] = mixed[h * TILE:(h + 1) * TILE]

        @pl.when(step < n - 1)
        def _():
            remote(step).start()

        return carry

    lax.fori_loop(0, n, one_tile, 0)
    own.start()

    def finish(step, carry):
        remote(step).wait()
        return carry

    lax.fori_loop(0, n - 1, finish, 0)
    own.wait()


def on_device(n, queries, keys, values, doc_lengths, tile_owner):
    tokens, width = queries.shape
    tiles = tokens // TILE
    heads = width // DH
    any_space = pl.BlockSpec(memory_space=pl.ANY)
    smem = pl.BlockSpec(memory_space=pltpu.SMEM)
    return pl.pallas_call(
        functools.partial(kernel, n, tiles, heads, 2),
        out_shape=jax.ShapeDtypeStruct((tokens, width), queries.dtype),
        in_specs=[any_space, any_space, any_space, smem, smem],
        out_specs=any_space,
        scratch_shapes=[
            pltpu.VMEM((tiles, TILE, width), queries.dtype),
            pltpu.VMEM((DOC_MOST // TILE + tiles, TILE, DH), keys.dtype),
            pltpu.VMEM((DOC_MOST // TILE + tiles, TILE, DH), values.dtype),
            pltpu.VMEM((n, TILE, width), queries.dtype),
            pltpu.VMEM((TILE, DOC_MOST + TILE), jnp.float32),
            pltpu.SemaphoreType.DMA((4,)),
            pltpu.SemaphoreType.DMA((2,)),
            pltpu.SemaphoreType.DMA((2,)),
            pltpu.SemaphoreType.DMA((n,)),
            pltpu.SemaphoreType.DMA((n,)),
        ],
        compiler_params=pltpu.CompilerParams(
            collective_id=0, has_side_effects=True, vmem_limit_bytes=48 << 20
        ),
    )(
        queries.reshape(tiles, TILE, width),
        keys.reshape(tiles, TILE, DH),
        values.reshape(tiles, TILE, DH),
        doc_lengths,
        tile_owner,
    )


def solution(mesh):
    return jax.shard_map(
        functools.partial(on_device, mesh.shape["ctx"]),
        mesh=mesh,
        in_specs=(
            P(("dp", "ctx"), None),
            P(("dp", "ctx"), None),
            P(("dp", "ctx"), None),
            P("dp"),
            P("dp"),
        ),
        out_specs=P(("dp", "ctx"), None),
        check_vma=False,
    )
```

```python
import functools

import jax
import jax.numpy as jnp
from jax import lax
from jax.experimental import pallas as pl
from jax.experimental.pallas import tpu as pltpu
from jax.sharding import PartitionSpec as P

TILE = 128
DOC_MOST = 1024
DH = 128
MESH = pl.DeviceIdType.MESH
LOG2E = 1.4426950408889634
MASKED = -1e30
ORDER = ((4, 0), (-3, 0), (3, 0), (-2, 0), (2, 0), (-1, 0), (1, 0), (4, 1), (-3, 1), (3, 1), (-2, 1), (2, 1), (-1, 1), (1, 1), (0, 1), (0, 0))


def kernel(
    n, tiles, heads, chunk, q_hbm, k_hbm, v_hbm, len_hbm, owner_hbm, out_hbm,
    q_all, k_ext, v_ext, stage, bias, len_ref, owner_ref, local_sem, halo_send, halo_recv, send_sem, recv_sem,
):
    dp = lax.axis_index("dp")
    me = lax.axis_index("ctx")
    tokens = tiles * TILE
    window = DOC_MOST + TILE
    reach = DOC_MOST // TILE

    loads = [
        pltpu.make_async_copy(len_hbm, len_ref, local_sem.at[3]),
        pltpu.make_async_copy(owner_hbm, owner_ref, local_sem.at[4]),
        pltpu.make_async_copy(q_hbm, q_all, local_sem.at[0]),
        pltpu.make_async_copy(k_hbm, k_ext.at[pl.ds(reach, tiles)], local_sem.at[1]),
        pltpu.make_async_copy(v_hbm, v_ext.at[pl.ds(reach, tiles)], local_sem.at[2]),
    ]
    for load in loads:
        load.start()

    barrier = pltpu.get_barrier_semaphore()
    for step in range(1, n):
        pl.semaphore_signal(
            barrier, inc=1, device_id=(dp, lax.rem(me + step, n)), device_id_type=MESH
        )
    pl.semaphore_wait(barrier, n - 1)

    following = (dp, lax.rem(me + 1, n))
    halos = [
        pltpu.make_async_remote_copy(
            src_ref=src.at[pl.ds(tiles - reach, reach)],
            dst_ref=dst.at[pl.ds(0, reach)],
            send_sem=halo_send.at[at],
            recv_sem=halo_recv.at[at],
            device_id=following,
            device_id_type=MESH,
        )
        for at, (src, dst) in enumerate(((k_hbm, k_ext), (v_hbm, v_ext)))
    ]
    for halo in halos:
        halo.start()

    loads[0].wait()
    lane = lax.broadcasted_iota(jnp.int32, (8, 128), 1)

    run, ends = jnp.int32(0), jnp.full((8, 128), 1 << 24, jnp.int32)
    for doc in range(len_ref.shape[0]):
        run = run + len_ref[doc]
        ends = jnp.where(lane == doc, run, ends)
    ends = ends.astype(jnp.float32)[0:1, :]

    for load in loads[1:]:
        load.wait()
    for halo in halos:
        halo.wait()

    row_in = lax.broadcasted_iota(jnp.int32, (TILE, 128), 0)
    key_at = lax.broadcasted_iota(jnp.int32, (TILE, window), 1) - DOC_MOST
    row_at = lax.broadcasted_iota(jnp.int32, (TILE, window), 0)

    def target(step):
        dz, flip = jnp.int32(ORDER[0][0]), jnp.int32(ORDER[0][1])
        for at, (hops, other) in enumerate(ORDER[1:], 1):
            dz, flip = jnp.where(step == at, hops, dz), jnp.where(step == at, other, flip)
        return ((me // 2 + dz + n // 2) % (n // 2)) * 2 + (me % 2 + flip) % 2

    def remote(step, part, size):
        return pltpu.make_async_remote_copy(
            src_ref=stage.at[step, pl.ds(part, size)],
            dst_ref=out_hbm.at[pl.ds(me * TILE + part, size)],
            send_sem=send_sem.at[step],
            recv_sem=recv_sem.at[step],
            device_id=(dp, target(step)),
            device_id_type=MESH,
        )

    own = pltpu.make_async_copy(
        stage.at[n - 1], out_hbm.at[pl.ds(me * TILE, TILE)], local_sem.at[5]
    )

    def one_tile(step, carry):
        tile = lax.rem(owner_ref[target(step) * n + me], tiles)
        base = (me * tokens + tile * TILE).astype(jnp.float32)
        begin = jnp.max(
            jnp.where(ends <= row_in.astype(jnp.float32) + base, ends, 0.0),
            axis=1, keepdims=True,
        )
        seen = (key_at <= row_at) & (key_at.astype(jnp.float32) + base >= begin)
        bias[...] = jnp.where(seen, 0.0, MASKED)

        k = jnp.concatenate([k_ext[tile + b] for b in range(reach + 1)], axis=0)
        v = jnp.concatenate([v_ext[tile + b] for b in range(reach + 1)], axis=0)
        for part in range(0, TILE, chunk):
            rows = pl.ds(part, chunk)
            q = jnp.concatenate(
                [q_all[tile, rows, pl.ds(h * DH, DH)] for h in range(heads)], axis=0
            )
            scores = lax.dot_general(
                q, k, (((1,), (1,)), ((), ())), preferred_element_type=jnp.float32
            )
            scores = scores * (LOG2E * DH ** -0.5) + jnp.concatenate([bias[rows]] * heads, axis=0)
            peak = jnp.max(scores, axis=1, keepdims=True)
            weights = jnp.exp2(scores - peak)
            total = jnp.sum(weights, axis=1, keepdims=True)
            mixed = jnp.dot(weights.astype(jnp.bfloat16), v, preferred_element_type=jnp.float32)
            mixed = (mixed / total).astype(jnp.bfloat16)
            for h in range(heads):
                stage[step, rows, pl.ds(h * DH, DH)] = mixed[h * chunk:(h + 1) * chunk]

            @pl.when(step < n - 1)
            def _():
                remote(step, part, chunk).start()

        return carry

    lax.fori_loop(0, n, one_tile, 0)
    own.start()

    def finish(step, carry):
        remote(step, 0, TILE).wait()
        return carry

    lax.fori_loop(0, n - 1, finish, 0)
    own.wait()


def on_device(n, queries, keys, values, doc_lengths, tile_owner):
    tokens, width = queries.shape
    tiles = tokens // TILE
    heads = width // DH
    hbm = pl.BlockSpec(memory_space=pltpu.HBM)
    return pl.pallas_call(
        functools.partial(kernel, n, tiles, heads, 32),
        out_shape=pltpu.VMEM((tokens, width), queries.dtype),
        in_specs=[hbm] * 5,
        out_specs=pl.BlockSpec(memory_space=pltpu.VMEM),
        scratch_shapes=[
            pltpu.VMEM((tiles, TILE, width), queries.dtype),
            pltpu.VMEM((DOC_MOST // TILE + tiles, TILE, DH), keys.dtype),
            pltpu.VMEM((DOC_MOST // TILE + tiles, TILE, DH), values.dtype),
            pltpu.VMEM((n, TILE, width), queries.dtype),
            pltpu.VMEM((TILE, DOC_MOST + TILE), jnp.float32),
            pltpu.SMEM(doc_lengths.shape, jnp.int32),
            pltpu.SMEM(tile_owner.shape, jnp.int32),
            pltpu.SemaphoreType.DMA((6,)),
            pltpu.SemaphoreType.DMA((2,)),
            pltpu.SemaphoreType.DMA((2,)),
            pltpu.SemaphoreType.DMA((n,)),
            pltpu.SemaphoreType.DMA((n,)),
        ],
        compiler_params=pltpu.CompilerParams(
            collective_id=0, has_side_effects=True, vmem_limit_bytes=32 << 20
        ),
    )(
        *(
            pltpu.with_memory_space_constraint(array, pltpu.HBM)
            for array in (
                queries.reshape(tiles, TILE, width),
                keys.reshape(tiles, TILE, DH),
                values.reshape(tiles, TILE, DH),
                doc_lengths,
                tile_owner,
            )
        )
    )


def solution(mesh):
    return jax.shard_map(
        functools.partial(on_device, mesh.shape["ctx"]),
        mesh=mesh,
        in_specs=(
            P(("dp", "ctx"), None),
            P(("dp", "ctx"), None),
            P(("dp", "ctx"), None),
            P("dp"),
            P("dp"),
        ),
        out_specs=P(("dp", "ctx"), None),
        check_vma=False,
    )
```

```python
import functools

import jax
import jax.numpy as jnp
from jax import lax
from jax.experimental import pallas as pl
from jax.experimental.pallas import tpu as pltpu
from jax.sharding import PartitionSpec as P

TILE = 128
DOC_MOST = 1024
DH = 128
MESH = pl.DeviceIdType.MESH
LOG2E = 1.4426950408889634
MASKED = -1e30
RELAYED = 16
RELAY_STEP = 5
ORDER = ((4, 0), (-3, 0), (3, 0), (-2, 0), (2, 0), (-1, 0), (1, 0), (4, 1), (-3, 1), (3, 1), (-2, 1), (2, 1), (-1, 1), (1, 1), (0, 1), (0, 0))


def kernel(
    n, tiles, heads, chunk, q_hbm, k_hbm, v_hbm, len_hbm, owner_hbm, out_hbm,
    q_all, k_ext, v_ext, stage, bias, len_ref, owner_ref, relay, local_sem, halo_send, halo_recv, send_sem, recv_sem,
    relay_sem,
):
    dp = lax.axis_index("dp")
    me = lax.axis_index("ctx")
    tokens = tiles * TILE
    window = DOC_MOST + TILE
    reach = DOC_MOST // TILE

    loads = [
        pltpu.make_async_copy(len_hbm, len_ref, local_sem.at[3]),
        pltpu.make_async_copy(owner_hbm, owner_ref, local_sem.at[4]),
        pltpu.make_async_copy(q_hbm, q_all, local_sem.at[0]),
        pltpu.make_async_copy(k_hbm, k_ext.at[pl.ds(reach, tiles)], local_sem.at[1]),
        pltpu.make_async_copy(v_hbm, v_ext.at[pl.ds(reach, tiles)], local_sem.at[2]),
    ]
    for load in loads:
        load.start()

    barrier = pltpu.get_barrier_semaphore()
    for step in range(1, n):
        pl.semaphore_signal(
            barrier, inc=1, device_id=(dp, lax.rem(me + step, n)), device_id_type=MESH
        )
    pl.semaphore_wait(barrier, n - 1)

    following = (dp, lax.rem(me + 1, n))
    halos = [
        pltpu.make_async_remote_copy(
            src_ref=src.at[pl.ds(tiles - reach, reach)],
            dst_ref=dst.at[pl.ds(0, reach)],
            send_sem=halo_send.at[at],
            recv_sem=halo_recv.at[at],
            device_id=following,
            device_id_type=MESH,
        )
        for at, (src, dst) in enumerate(((k_hbm, k_ext), (v_hbm, v_ext)))
    ]
    for halo in halos:
        halo.start()

    loads[0].wait()
    lane = lax.broadcasted_iota(jnp.int32, (8, 128), 1)

    run, ends = jnp.int32(0), jnp.full((8, 128), 1 << 24, jnp.int32)
    for doc in range(len_ref.shape[0]):
        run = run + len_ref[doc]
        ends = jnp.where(lane == doc, run, ends)
    ends = ends.astype(jnp.float32)[0:1, :]

    for load in loads[1:]:
        load.wait()
    for halo in halos:
        halo.wait_recv()

    row_in = lax.broadcasted_iota(jnp.int32, (TILE, 128), 0)
    key_at = lax.broadcasted_iota(jnp.int32, (TILE, window), 1) - DOC_MOST
    row_at = lax.broadcasted_iota(jnp.int32, (TILE, window), 0)

    def target(source, step):
        dz, flip = jnp.int32(ORDER[0][0]), jnp.int32(ORDER[0][1])
        for at, (hops, other) in enumerate(ORDER[1:], 1):
            dz, flip = jnp.where(step == at, hops, dz), jnp.where(step == at, other, flip)
        return ((source // 2 + dz + n // 2) % (n // 2)) * 2 + (source % 2 + flip) % 2

    def remote(step, part, size):
        return pltpu.make_async_remote_copy(
            src_ref=stage.at[step, pl.ds(part, size)],
            dst_ref=out_hbm.at[pl.ds(me * TILE + part, size)],
            send_sem=send_sem.at[step],
            recv_sem=recv_sem.at[step],
            device_id=(dp, target(me, step)),
            device_id_type=MESH,
        )

    detours = (me // 2) % 2 == 0
    relays = (me // 2) % 2 == 1
    direct = TILE - RELAYED
    to_relay = pltpu.make_async_remote_copy(
        src_ref=stage.at[0, pl.ds(direct, RELAYED)],
        dst_ref=relay,
        send_sem=send_sem.at[0],
        recv_sem=relay_sem.at[0],
        device_id=(dp, lax.rem(me + n - 2, n)),
        device_id_type=MESH,
    )
    source = lax.rem(me + 2, n)
    onward = pltpu.make_async_remote_copy(
        src_ref=relay,
        dst_ref=out_hbm.at[pl.ds(source * TILE + direct, RELAYED)],
        send_sem=relay_sem.at[1],
        recv_sem=recv_sem.at[0],
        device_id=(dp, target(source, 0)),
        device_id_type=MESH,
    )

    own = pltpu.make_async_copy(
        stage.at[n - 1], out_hbm.at[pl.ds(me * TILE, TILE)], local_sem.at[5]
    )

    def one_tile(step, carry):
        tile = lax.rem(owner_ref[target(me, step) * n + me], tiles)
        base = (me * tokens + tile * TILE).astype(jnp.float32)
        begin = jnp.max(
            jnp.where(ends <= row_in.astype(jnp.float32) + base, ends, 0.0),
            axis=1, keepdims=True,
        )
        seen = (key_at <= row_at) & (key_at.astype(jnp.float32) + base >= begin)
        bias[...] = jnp.where(seen, 0.0, MASKED)

        k = jnp.concatenate([k_ext[tile + b] for b in range(reach + 1)], axis=0)
        v = jnp.concatenate([v_ext[tile + b] for b in range(reach + 1)], axis=0)
        for part in range(0, TILE, chunk):
            rows = pl.ds(part, chunk)
            q = jnp.concatenate(
                [q_all[tile, rows, pl.ds(h * DH, DH)] for h in range(heads)], axis=0
            )
            scores = lax.dot_general(
                q, k, (((1,), (1,)), ((), ())), preferred_element_type=jnp.float32
            )
            scores = scores * (LOG2E * DH ** -0.5) + jnp.concatenate([bias[rows]] * heads, axis=0)
            peak = jnp.max(scores, axis=1, keepdims=True)
            weights = jnp.exp2(scores - peak)
            total = jnp.sum(weights, axis=1, keepdims=True)
            mixed = jnp.dot(weights.astype(jnp.bfloat16), v, preferred_element_type=jnp.float32)
            mixed = (mixed / total).astype(jnp.bfloat16)
            for h in range(heads):
                stage[step, rows, pl.ds(h * DH, DH)] = mixed[h * chunk:(h + 1) * chunk]

            if part + chunk < TILE:
                @pl.when(step < n - 1)
                def _():
                    remote(step, part, chunk).start()
            else:
                @pl.when((step < n - 1) & ((step > 0) | relays))
                def _():
                    remote(step, part, chunk).start()

                @pl.when((step == 0) & detours)
                def _():
                    if part < direct:
                        remote(step, part, direct - part).start()
                    to_relay.start()

        @pl.when((step == RELAY_STEP) & relays)
        def _():
            to_relay.wait_recv()
            onward.start()

        return carry

    lax.fori_loop(0, n, one_tile, 0)
    own.start()
    for halo in halos:
        halo.wait_send()

    def finish(step, carry):
        remote(step, 0, TILE).wait()
        return carry

    lax.fori_loop(0, n - 1, finish, 0)
    own.wait()

    @pl.when(relays)
    def _():
        onward.wait_send()


def on_device(n, queries, keys, values, doc_lengths, tile_owner):
    tokens, width = queries.shape
    tiles = tokens // TILE
    heads = width // DH
    hbm = pl.BlockSpec(memory_space=pltpu.HBM)
    return pl.pallas_call(
        functools.partial(kernel, n, tiles, heads, 32),
        out_shape=pltpu.VMEM((tokens, width), queries.dtype),
        in_specs=[hbm] * 5,
        out_specs=pl.BlockSpec(memory_space=pltpu.VMEM),
        scratch_shapes=[
            pltpu.VMEM((tiles, TILE, width), queries.dtype),
            pltpu.VMEM((DOC_MOST // TILE + tiles, TILE, DH), keys.dtype),
            pltpu.VMEM((DOC_MOST // TILE + tiles, TILE, DH), values.dtype),
            pltpu.VMEM((n, TILE, width), queries.dtype),
            pltpu.VMEM((TILE, DOC_MOST + TILE), jnp.float32),
            pltpu.SMEM(doc_lengths.shape, jnp.int32),
            pltpu.SMEM(tile_owner.shape, jnp.int32),
            pltpu.VMEM((RELAYED, width), queries.dtype),
            pltpu.SemaphoreType.DMA((6,)),
            pltpu.SemaphoreType.DMA((2,)),
            pltpu.SemaphoreType.DMA((2,)),
            pltpu.SemaphoreType.DMA((n,)),
            pltpu.SemaphoreType.DMA((n,)),
            pltpu.SemaphoreType.DMA((2,)),
        ],
        compiler_params=pltpu.CompilerParams(
            collective_id=0, has_side_effects=True, vmem_limit_bytes=32 << 20
        ),
    )(
        *(
            pltpu.with_memory_space_constraint(array, pltpu.HBM)
            for array in (
                queries.reshape(tiles, TILE, width),
                keys.reshape(tiles, TILE, DH),
                values.reshape(tiles, TILE, DH),
                doc_lengths,
                tile_owner,
            )
        )
    )


def solution(mesh):
    return jax.shard_map(
        functools.partial(on_device, mesh.shape["ctx"]),
        mesh=mesh,
        in_specs=(
            P(("dp", "ctx"), None),
            P(("dp", "ctx"), None),
            P(("dp", "ctx"), None),
            P("dp"),
            P("dp"),
        ),
        out_specs=P(("dp", "ctx"), None),
        check_vma=False,
    )
```

```python
import functools

import jax
import jax.numpy as jnp
from jax import lax
from jax.experimental import pallas as pl
from jax.experimental.pallas import tpu as pltpu
from jax.sharding import PartitionSpec as P

TILE = 128
DOC_MOST = 1024
DH = 128
MESH = pl.DeviceIdType.MESH
LOG2E = 1.4426950408889634
MASKED = -1e30
RELAYED = 16
RELAY_STEP = 5
ORDER = ((4, 0), (-3, 0), (3, 0), (-2, 0), (2, 0), (-1, 0), (1, 0), (4, 1), (-3, 1), (3, 1), (-2, 1), (2, 1), (-1, 1), (1, 1), (0, 1), (0, 0))


def kernel(
    n, tiles, heads, chunk, q_hbm, k_hbm, v_hbm, len_hbm, owner_hbm, out_hbm,
    q_all, k_ext, v_ext, stage, bias, len_ref, owner_ref, relay, local_sem, halo_send, halo_recv, send_sem, recv_sem,
    relay_sem,
):
    dp = lax.axis_index("dp")
    me = lax.axis_index("ctx")
    tokens = tiles * TILE
    window = DOC_MOST + TILE
    reach = DOC_MOST // TILE

    loads = [
        pltpu.make_async_copy(len_hbm, len_ref, local_sem.at[3]),
        pltpu.make_async_copy(owner_hbm, owner_ref, local_sem.at[4]),
        pltpu.make_async_copy(q_hbm, q_all, local_sem.at[0]),
        pltpu.make_async_copy(k_hbm, k_ext.at[pl.ds(reach, tiles)], local_sem.at[1]),
        pltpu.make_async_copy(v_hbm, v_ext.at[pl.ds(reach, tiles)], local_sem.at[2]),
    ]
    for load in loads:
        load.start()

    barrier = pltpu.get_barrier_semaphore()
    for step in sorted(range(1, n), key=lambda step: abs(step - n // 2)):
        pl.semaphore_signal(
            barrier, inc=1, device_id=(dp, lax.rem(me + step, n)), device_id_type=MESH
        )
    loads[0].wait()
    lane = lax.broadcasted_iota(jnp.int32, (8, 128), 1)

    run, ends = jnp.int32(0), jnp.full((8, 128), 1 << 24, jnp.int32)
    for doc in range(len_ref.shape[0]):
        run = run + len_ref[doc]
        ends = jnp.where(lane == doc, run, ends)
    ends = ends.astype(jnp.float32)[0:1, :]

    pl.semaphore_wait(barrier, n - 1)

    following = (dp, lax.rem(me + 1, n))
    halos = [
        pltpu.make_async_remote_copy(
            src_ref=src.at[pl.ds(tiles - reach, reach)],
            dst_ref=dst.at[pl.ds(0, reach)],
            send_sem=halo_send.at[at],
            recv_sem=halo_recv.at[at],
            device_id=following,
            device_id_type=MESH,
        )
        for at, (src, dst) in enumerate(((k_hbm, k_ext), (v_hbm, v_ext)))
    ]
    for halo in halos:
        halo.start()

    for load in loads[1:]:
        load.wait()

    row_in = lax.broadcasted_iota(jnp.int32, (TILE, 128), 0)
    key_at = lax.broadcasted_iota(jnp.int32, (TILE, window), 1) - DOC_MOST
    row_at = lax.broadcasted_iota(jnp.int32, (TILE, window), 0)

    def target(source, step):
        dz, flip = jnp.int32(ORDER[0][0]), jnp.int32(ORDER[0][1])
        for at, (hops, other) in enumerate(ORDER[1:], 1):
            dz, flip = jnp.where(step == at, hops, dz), jnp.where(step == at, other, flip)
        return ((source // 2 + dz + n // 2) % (n // 2)) * 2 + (source % 2 + flip) % 2

    def remote(step, part, size):
        return pltpu.make_async_remote_copy(
            src_ref=stage.at[step, pl.ds(part, size)],
            dst_ref=out_hbm.at[pl.ds(me * TILE + part, size)],
            send_sem=send_sem.at[step],
            recv_sem=recv_sem.at[step],
            device_id=(dp, target(me, step)),
            device_id_type=MESH,
        )

    detours = (me // 2) % 2 == 0
    relays = (me // 2) % 2 == 1
    direct = TILE - RELAYED
    to_relay = pltpu.make_async_remote_copy(
        src_ref=stage.at[0, pl.ds(direct, RELAYED)],
        dst_ref=relay,
        send_sem=send_sem.at[0],
        recv_sem=relay_sem.at[0],
        device_id=(dp, lax.rem(me + n - 2, n)),
        device_id_type=MESH,
    )
    source = lax.rem(me + 2, n)
    onward = pltpu.make_async_remote_copy(
        src_ref=relay,
        dst_ref=out_hbm.at[pl.ds(source * TILE + direct, RELAYED)],
        send_sem=relay_sem.at[1],
        recv_sem=recv_sem.at[0],
        device_id=(dp, target(source, 0)),
        device_id_type=MESH,
    )

    own = pltpu.make_async_copy(
        stage.at[n - 1], out_hbm.at[pl.ds(me * TILE, TILE)], local_sem.at[5]
    )

    def tile_of(step):
        return lax.rem(owner_ref[target(me, step) * n + me], tiles)

    def make_bias(step):
        base = (me * tokens + tile_of(step) * TILE).astype(jnp.float32)
        begin = jnp.max(
            jnp.where(ends <= row_in.astype(jnp.float32) + base, ends, 0.0),
            axis=1, keepdims=True,
        )
        seen = (key_at <= row_at) & (key_at.astype(jnp.float32) + base >= begin)
        bias[...] = jnp.where(seen, 0.0, MASKED)

    make_bias(0)
    halos[0].wait_recv()

    def one_tile(step, carry):
        tile = tile_of(step)
        k = jnp.concatenate([k_ext[tile + b] for b in range(reach + 1)], axis=0)
        for part in range(0, TILE, chunk):
            rows = pl.ds(part, chunk)
            q = jnp.concatenate(
                [q_all[tile, rows, pl.ds(h * DH, DH)] for h in range(heads)], axis=0
            )
            scores = lax.dot_general(
                q, k, (((1,), (1,)), ((), ())), preferred_element_type=jnp.float32
            )
            scores = scores * (LOG2E * DH ** -0.5) + jnp.concatenate([bias[rows]] * heads, axis=0)
            peak = jnp.max(scores, axis=1, keepdims=True)
            weights = jnp.exp2(scores - peak)
            total = jnp.sum(weights, axis=1, keepdims=True)
            if part == 0:
                @pl.when(step == 0)
                def _():
                    halos[1].wait_recv()

            v = jnp.concatenate([v_ext[tile + b] for b in range(reach + 1)], axis=0)
            mixed = jnp.dot(weights.astype(jnp.bfloat16), v, preferred_element_type=jnp.float32)
            mixed = (mixed / total).astype(jnp.bfloat16)
            for h in range(heads):
                stage[step, rows, pl.ds(h * DH, DH)] = mixed[h * chunk:(h + 1) * chunk]

            if part + chunk < TILE:
                @pl.when(step < n - 1)
                def _():
                    remote(step, part, chunk).start()
            else:
                @pl.when((step < n - 1) & ((step > 0) | relays))
                def _():
                    remote(step, part, chunk).start()

                @pl.when((step == 0) & detours)
                def _():
                    if part < direct:
                        remote(step, part, direct - part).start()
                    to_relay.start()

        @pl.when((step == RELAY_STEP) & relays)
        def _():
            to_relay.wait_recv()
            onward.start()

        make_bias(lax.rem(step + 1, n))
        return carry

    lax.fori_loop(0, n, one_tile, 0)
    own.start()
    for halo in halos:
        halo.wait_send()

    def finish(step, carry):
        remote(step, 0, TILE).wait()
        return carry

    lax.fori_loop(0, n - 1, finish, 0)
    own.wait()

    @pl.when(relays)
    def _():
        onward.wait_send()


def on_device(n, queries, keys, values, doc_lengths, tile_owner):
    tokens, width = queries.shape
    tiles = tokens // TILE
    heads = width // DH
    hbm = pl.BlockSpec(memory_space=pltpu.HBM)
    return pl.pallas_call(
        functools.partial(kernel, n, tiles, heads, 16),
        out_shape=pltpu.VMEM((tokens, width), queries.dtype),
        in_specs=[hbm] * 5,
        out_specs=pl.BlockSpec(memory_space=pltpu.VMEM),
        scratch_shapes=[
            pltpu.VMEM((tiles, TILE, width), queries.dtype),
            pltpu.VMEM((DOC_MOST // TILE + tiles, TILE, DH), keys.dtype),
            pltpu.VMEM((DOC_MOST // TILE + tiles, TILE, DH), values.dtype),
            pltpu.VMEM((n, TILE, width), queries.dtype),
            pltpu.VMEM((TILE, DOC_MOST + TILE), jnp.float32),
            pltpu.SMEM(doc_lengths.shape, jnp.int32),
            pltpu.SMEM(tile_owner.shape, jnp.int32),
            pltpu.VMEM((RELAYED, width), queries.dtype),
            pltpu.SemaphoreType.DMA((6,)),
            pltpu.SemaphoreType.DMA((2,)),
            pltpu.SemaphoreType.DMA((2,)),
            pltpu.SemaphoreType.DMA((n,)),
            pltpu.SemaphoreType.DMA((n,)),
            pltpu.SemaphoreType.DMA((2,)),
        ],
        compiler_params=pltpu.CompilerParams(
            collective_id=0, has_side_effects=True, vmem_limit_bytes=32 << 20
        ),
    )(
        *(
            pltpu.with_memory_space_constraint(array, pltpu.HBM)
            for array in (
                queries.reshape(tiles, TILE, width),
                keys.reshape(tiles, TILE, DH),
                values.reshape(tiles, TILE, DH),
                doc_lengths,
                tile_owner,
            )
        )
    )


def solution(mesh):
    return jax.shard_map(
        functools.partial(on_device, mesh.shape["ctx"]),
        mesh=mesh,
        in_specs=(
            P(("dp", "ctx"), None),
            P(("dp", "ctx"), None),
            P(("dp", "ctx"), None),
            P("dp"),
            P("dp"),
        ),
        out_specs=P(("dp", "ctx"), None),
        check_vma=False,
    )
```
